32 devices in a mesh: groups: 2 (over y), replica: 4 (over z), tensor: 4 (over x, core).
Axes of the slice: x: 2, y: 2, z: 4, core: 2. Of those that a mesh axis runs over, the one named last changes fastest.
Arguments:
- queries: bfloat16 [2, 256, 4, 512], P(None, ('groups', 'replica'), 'tensor'), parts along dimension 1, may hold values from -130 to 130
- key_cache: bfloat16 [256, 4, 16, 128], P(('groups', 'replica'), 'tensor'), parts along dimension 0, may hold values from -6 to 6
- value_cache: bfloat16 [256, 4, 16, 128], P(('groups', 'replica'), 'tensor'), parts along dimension 0, may hold values from -6 to 6
- decoded_keys: bfloat16 [2, 256, 4, 128], P(None, ('groups', 'replica'), 'tensor'), parts along dimension 1, may hold values from -6 to 6
- decoded_values: bfloat16 [2, 256, 4, 128], P(None, ('groups', 'replica'), 'tensor'), parts along dimension 1, may hold values from -6 to 6
- lengths: int32 [256], P(('groups', 'replica')), parts along dimension 0, may hold values from 1 to 16, 1024 in all
- request_adapters: int32 [256], P(('groups', 'replica')), parts along dimension 0, may hold values from 0 to 31, as said below
- table_row_of: int32 [64], P('groups'), parts along dimension 0, may hold values from 0 to 31, as said below
- output_matrix: bfloat16 [2048, 4096], P('tensor'), may hold values from -0.125 to 0.125
- down_maps: bfloat16 [32, 4, 512, 16], P('replica', 'tensor'), may hold values from -0.125 to 0.125
- up_maps: bfloat16 [32, 16, 4096], P('replica', None, 'tensor'), may hold values from -1.5 to 1.5
Outputs:
- projected: bfloat16 [2, 256, 4096], P(None, ('groups', 'replica'), 'tensor'), parts along dimension 1
The draws below stay inside these ranges and needn't reach their ends.
There are 2 independent parts, one for each index of `groups`. The reference program is written for one: setup_inputs(seed, part) draws one part's arguments, and reference() takes and returns one part's arrays. A program takes and returns all parts, laid end to end along the dimension named above; an argument that names none is the same for every part. Nothing has to cross between parts.
Inputs may be any that keep to these rules, and one draw needn't show every extreme that they name: table_row_of is a permutation; adapter a lies with replica table_row_of[a] // 8. `request_adapters`: among the 32 requests of one replica (aligned blocks), at most 16 name adapters that lie with the same replica, and in every block some replica is named exactly 16 times.
All inputs are finite; a program needn't handle non-finite values. No bound on the sum of `lengths` on one device may be relied on, other than what follows from the above.
Results may differ from the reference program's by a relative error of at most 0.008.
Values may be sent and summed in bfloat16 or wider, within the bound.
A program may use at most 64 MiB of HBM per device.

```python
import math
import jax
import jax.numpy as jnp
import numpy as np
from jax import lax

HEAD_SIZE = 128
QUERY_PER_KEY = 4
ADAPTER_RANK = 16
OUTPUT_FEATURES = 4096
STEPS = 2
CACHE = 16
ADP_DEV = 8
REPLICA_ROWS = 32
KEY_VALUE_HEADS = 4
ROWS = 128
ADAPTER_TOTAL = 32
CAP = 16
N_REPLICA = 4


def shared_keys(key):
    return jnp.clip(jax.random.normal(jax.random.fold_in(key, 101), (ROWS, KEY_VALUE_HEADS, CACHE, HEAD_SIZE), jnp.float32), -6.0, 6.0)


def storage_order(key):
    return jax.random.permutation(jax.random.fold_in(key, 202), ADAPTER_TOTAL)


def draw_key_cache(key, part):
    keys = shared_keys(key)
    return keys.astype(jnp.bfloat16)


def draw_queries(key, part):
    key = jax.random.fold_in(key, 7)
    values = jnp.clip(jax.random.normal(key, (STEPS, ROWS, KEY_VALUE_HEADS, QUERY_PER_KEY, HEAD_SIZE), jnp.float32), -6.0, 6.0)
    return values.reshape(STEPS, ROWS, KEY_VALUE_HEADS, QUERY_PER_KEY * HEAD_SIZE).astype(jnp.bfloat16)


def draw_table_row_of(key, part):
    return storage_order(key).astype(jnp.int32)


def draw_request_adapters(key, part):
    order = storage_order(key).astype(jnp.int32)
    inverse = jnp.zeros((ADAPTER_TOTAL,), jnp.int32).at[order].set(jnp.arange(ADAPTER_TOTAL, dtype=jnp.int32))
    key = jax.random.fold_in(key, 3)
    spots = N_REPLICA * CAP

    def one_block(index):
        block_key = jax.random.fold_in(key, index)
        owners = (jax.random.permutation(jax.random.fold_in(block_key, 1), spots) // CAP).astype(jnp.int32)
        hottest = owners[0]
        score = jnp.where(owners == hottest, 0, 1) * spots + jnp.arange(spots, dtype=jnp.int32)
        owners = owners[jnp.argsort(score, stable=True)][:REPLICA_ROWS]
        owners = jax.random.permutation(jax.random.fold_in(block_key, 2), owners)
        local = jax.random.randint(jax.random.fold_in(block_key, 3), (REPLICA_ROWS,), 0, ADP_DEV)
        return inverse[owners * ADP_DEV + local]
    return jax.vmap(one_block)(jnp.arange(N_REPLICA, dtype=jnp.int32)).reshape(ROWS).astype(jnp.int32)


def steps_of(stream_key, dims, cuts, smallest, high):
    def one(position, blocks):
        steps = jax.random.uniform(jax.random.fold_in(jax.random.fold_in(stream_key, 6), position), (blocks,), jnp.float32, smallest / len(cuts), high / len(cuts))
        return jnp.repeat(jnp.exp(steps), dims[position] // blocks).reshape((-1,) + (1,) * (len(dims) - position - 1))

    factor_of = one(*cuts[0])
    for cut in cuts[1:]:
        factor_of = factor_of * one(*cut)
    return factor_of


def profile(count, total, limit, skew):
    weights = [(1 << 20) // math.isqrt(grade ** skew) + 1 for grade in range(2, count + 1)]
    surplus, given = total - limit - (count - 1), [1] * (count - 1)
    while surplus > 0:
        free = [i for i in range(count - 1) if given[i] < limit]
        whole, left = sum([weights[i] for i in free]), surplus
        for i in free:
            more = min(limit - given[i], max(1, left * weights[i] // whole), surplus)
            given[i] = given[i] + more
            surplus = surplus - more
    return np.array([limit] + given)


def ragged(own_key, amount, total, reach, lean):
    if amount == 2:
        one = jax.random.randint(own_key, (), max(1, total - reach), min(reach, total - 1) + 1)
        return jnp.stack([one, total - one])
    sizes = jnp.asarray(profile(amount, total, reach, lean), jnp.int32)
    couples = (amount - 1) // 2
    donor, taker = sizes[1:1 + 2 * couples:2], sizes[2:2 + 2 * couples:2]
    room = jnp.minimum(donor - 1, reach - taker)
    shifted = jax.random.randint(jax.random.fold_in(own_key, 1), (couples,), 0, 1 << 20) % (room + 1)
    sizes = sizes.at[1:1 + 2 * couples:2].set(donor - shifted).at[2:2 + 2 * couples:2].set(taker + shifted)
    return sizes[jax.random.permutation(jax.random.fold_in(own_key, 2), amount)]


def centred(stream_key, extent, spread, reach, shards=(), kind=jnp.bfloat16):
    values = jax.random.normal(stream_key, extent, jnp.float32) * spread
    if len(shards) > 0:
        values = steps_of(stream_key, extent, shards, -0.22, 0.18) * values
    return jnp.clip(values, min=-reach, max=reach).astype(kind)


def setup_inputs(seed: int = 0, part: int = 0) -> dict:
    streams_of = jax.random.split(jax.random.key(seed), 12)
    part_keys = jax.random.split(jax.random.fold_in(streams_of[11], part), 12)
    queries = draw_queries(jax.random.fold_in(jax.random.fold_in(streams_of[11], part), 71), part)
    key_cache = draw_key_cache(jax.random.fold_in(jax.random.fold_in(streams_of[11], part), 71), part)
    value_cache = centred(part_keys[2], (ROWS, KEY_VALUE_HEADS, CACHE, HEAD_SIZE), 1.0, 6.0, ((0, 4), (1, 4)))
    decoded_keys = centred(part_keys[3], (STEPS, ROWS, KEY_VALUE_HEADS, HEAD_SIZE), 1.0, 6.0, ((1, 4), (2, 4)))
    decoded_values = centred(part_keys[4], (STEPS, ROWS, KEY_VALUE_HEADS, HEAD_SIZE), 1.0, 6.0, ((1, 4), (2, 4)))
    lengths = ragged(part_keys[5], ROWS, ROWS * CACHE // 2, CACHE, 0).astype(jnp.int32)
    request_adapters = draw_request_adapters(jax.random.fold_in(jax.random.fold_in(streams_of[11], part), 71), part)
    table_row_of = draw_table_row_of(jax.random.fold_in(jax.random.fold_in(streams_of[11], part), 71), part)
    output_matrix = centred(streams_of[8], (KEY_VALUE_HEADS * QUERY_PER_KEY * HEAD_SIZE, OUTPUT_FEATURES), (KEY_VALUE_HEADS * QUERY_PER_KEY * HEAD_SIZE) ** -0.5, 0.125, ((0, 4),))
    down_maps = centred(streams_of[9], (ADAPTER_TOTAL, KEY_VALUE_HEADS, QUERY_PER_KEY * HEAD_SIZE, ADAPTER_RANK), (KEY_VALUE_HEADS * QUERY_PER_KEY * HEAD_SIZE) ** -0.5, 0.125, ((0, 4), (1, 4)))
    up_maps = centred(streams_of[10], (ADAPTER_TOTAL, ADAPTER_RANK, OUTPUT_FEATURES), ADAPTER_RANK ** -0.5, 1.5, ((0, 4), (2, 4)))
    return dict(queries=queries, key_cache=key_cache, value_cache=value_cache, decoded_keys=decoded_keys, decoded_values=decoded_values, lengths=lengths, request_adapters=request_adapters, table_row_of=table_row_of, output_matrix=output_matrix, down_maps=down_maps, up_maps=up_maps)


ADAPTER_SCALE = 2.0

def reference(queries, key_cache, value_cache, decoded_keys, decoded_values, lengths, request_adapters, table_row_of, output_matrix, down_maps, up_maps):
    scale = 1.0 / math.sqrt(HEAD_SIZE)
    query = queries.astype(jnp.float32).reshape(STEPS, ROWS, KEY_VALUE_HEADS, QUERY_PER_KEY, HEAD_SIZE)
    cached = jnp.einsum('srgjd,rgpd->srgjp', query, key_cache.astype(jnp.float32)) * scale
    valid = jnp.arange(CACHE, dtype=jnp.int32)[None, :] < lengths[:, None]
    cached = jnp.where(valid[None, :, None, None, :], cached, -jnp.inf)
    fresh = jnp.einsum('srgjd,trgd->srgjt', query, decoded_keys.astype(jnp.float32)) * scale
    causal = jnp.arange(STEPS, dtype=jnp.int32)[None, :] <= jnp.arange(STEPS, dtype=jnp.int32)[:, None]
    fresh = jnp.where(causal[:, None, None, None, :], fresh, -jnp.inf)
    top = jnp.maximum(lax.optimization_barrier(jnp.max(cached, axis=-1)), lax.optimization_barrier(jnp.max(fresh, axis=-1)))
    exp_cached = jnp.exp(cached - top[..., None])
    exp_fresh = jnp.exp(fresh - top[..., None])
    total = lax.optimization_barrier(jnp.sum(exp_cached, axis=-1)) + lax.optimization_barrier(jnp.sum(exp_fresh, axis=-1))
    weight_cached = (exp_cached / total[..., None]).astype(jnp.bfloat16)
    weight_fresh = (exp_fresh / total[..., None]).astype(jnp.bfloat16)
    mixed = jnp.einsum('srgjp,rgpd->srgjd', weight_cached.astype(jnp.float32), value_cache.astype(jnp.float32))
    mixed = mixed + jnp.einsum('srgjt,trgd->srgjd', weight_fresh.astype(jnp.float32), decoded_values.astype(jnp.float32))
    heads = mixed.astype(jnp.bfloat16).reshape(STEPS * ROWS, KEY_VALUE_HEADS * QUERY_PER_KEY * HEAD_SIZE)
    base = jnp.dot(heads, output_matrix, preferred_element_type=jnp.float32).reshape(STEPS, ROWS, OUTPUT_FEATURES)
    stored = table_row_of[request_adapters]
    grouped = heads.reshape(STEPS, ROWS, KEY_VALUE_HEADS * QUERY_PER_KEY * HEAD_SIZE)

    def block(index):
        start = index * REPLICA_ROWS
        rows_of_block = lax.dynamic_slice_in_dim(stored, start, REPLICA_ROWS)
        block_heads = lax.dynamic_slice_in_dim(grouped, start, REPLICA_ROWS, 1).astype(jnp.float32)
        down_rows = down_maps[rows_of_block].reshape(REPLICA_ROWS, KEY_VALUE_HEADS * QUERY_PER_KEY * HEAD_SIZE, ADAPTER_RANK).astype(jnp.float32)
        up_rows = up_maps[rows_of_block].astype(jnp.float32)
        lower_product = jnp.einsum('srh,rhk->srk', block_heads, down_rows, precision=lax.Precision.HIGHEST)
        return (ADAPTER_SCALE * jnp.einsum('gyd,ydh->gyh', lower_product, up_rows, precision=lax.Precision.HIGHEST)).astype(jnp.bfloat16)
    deltas = lax.map(block, jnp.arange(N_REPLICA, dtype=jnp.int32))
    delta = jnp.transpose(deltas, (1, 0, 2, 3)).reshape(STEPS, ROWS, OUTPUT_FEATURES)
    return (base + delta.astype(jnp.float32)).astype(jnp.bfloat16)
```

```python
import functools
import math

import jax
import jax.numpy as jnp
from jax import lax
from jax.experimental import pallas as pl
from jax.experimental.pallas import tpu as pltpu
from jax.sharding import PartitionSpec as P

ADAPTER_SCALE = 2.0
MASKED = -1e30
MESH = pl.DeviceIdType.MESH
F32 = jnp.float32
BF16 = jnp.bfloat16


def iota(shape, dim):
    return lax.broadcasted_iota(jnp.int32, shape, dim)


def dot(a, b):
    return jnp.dot(a, b, preferred_element_type=F32)


def dot_t(a, b):
    return lax.dot_general(a, b, (((1,), (1,)), ((), ())), preferred_element_type=F32)


def aligned(start, size):
    return pl.ds(pl.multiple_of(start * size, size), size)


def to_column(row):
    n = row.shape[1]
    eye = iota((n, n), 0) == iota((n, n), 1)
    return jnp.sum(jnp.where(eye, row, 0.0), axis=1, keepdims=True)


def to_row(column):
    n = column.shape[0]
    eye = iota((n, n), 0) == iota((n, n), 1)
    return jnp.sum(jnp.where(eye, column, 0.0), axis=0, keepdims=True)


def each(count, body):
    if count <= 8:
        for i in range(count):
            body(i)
    else:
        lax.fori_loop(0, count, lambda i, c: (body(i), c)[1], 0)


def kernel(
    dims,
    lengths_ref,
    adapters_ref,
    table_ref,
    query_hbm,
    key_hbm,
    value_hbm,
    new_key_hbm,
    new_value_hbm,
    matrix_hbm,
    down_hbm,
    up_hbm,
    out_ref,
    query,
    keys,
    values,
    matrix,
    down,
    up,
    heads,
    heads_out,
    heads_in,
    mask_out,
    mask_in,
    low_out,
    low_in,
    delta_out,
    delta_in,
    base_own,
    base_out,
    base_in,
    local_sem,
    mask_send,
    mask_recv,
    heads_send,
    heads_recv,
    low_send,
    low_recv,
    delta_send,
    delta_recv,
    base_send,
    base_recv,
):
    steps, rows, cache, head, owners, tensors, share, rank, cap, chunk = dims
    me = lax.axis_index("replica")
    mine = lax.axis_index("tensor")
    columns = out_ref.shape[1]
    cached = rows * cache
    per_group = query.shape[1] // head

    def ring(off):
        return lax.rem(me + off, owners)

    def back(off):
        return lax.rem(me + owners - off, owners)

    def peer(k):
        if tensors % 2:
            return lax.rem(mine + k, tensors)
        flipped = mine // 2 * 2 + (mine % 2 + k % 2) % 2
        return (flipped + k // 2 * 2) % tensors

    barrier = pltpu.get_barrier_semaphore()

    def greet(i):
        pl.semaphore_signal(
            barrier, inc=1, device_id={"replica": ring(i + 1)}, device_id_type=MESH
        )

    each(owners - 1, greet)
    for k in range(1, tensors):
        pl.semaphore_signal(barrier, inc=1, device_id={"tensor": peer(k)}, device_id_type=MESH)

    loads = [
        (query_hbm, query),
        (key_hbm, keys.at[pl.ds(0, cached)]),
        (new_key_hbm, keys.at[pl.ds(cached, steps * rows)]),
        (value_hbm, values.at[pl.ds(0, cached)]),
        (new_value_hbm, values.at[pl.ds(cached, steps * rows)]),
        (down_hbm, down),
        (matrix_hbm, matrix),
        (up_hbm, up),
    ]
    loads = [pltpu.make_async_copy(a, b, local_sem.at[i]) for i, (a, b) in enumerate(loads)]
    for load in loads:
        load.start()

    wanted = to_column(adapters_ref[...].astype(F32))
    total = table_ref.shape[1]
    hit = wanted == iota((rows, total), 1).astype(F32)
    stored = jnp.sum(jnp.where(hit, table_ref[...].astype(F32), 0.0), axis=1, keepdims=True)
    owner = jnp.floor((stored + 0.5) / share)
    local = stored - owner * share
    owner_row = to_row(owner)
    earlier = iota((rows, rows), 1) < iota((rows, rows), 0)
    rank_in = jnp.sum(
        jnp.where(earlier & (owner == owner_row), 1.0, 0.0), axis=1, keepdims=True
    )
    slot = owner * chunk + rank_in
    slot_row = to_row(slot)
    places = owners * chunk
    place_row = iota((places, rows), 0).astype(F32)
    place_col = iota((rows, places), 1).astype(F32)
    pick = [
        jnp.where(place_row == slot_row + s * cap, 1.0, 0.0).astype(BF16) for s in range(steps)
    ]
    unpick = [
        jnp.where(place_col == slot + s * cap, 1.0, 0.0).astype(BF16) for s in range(steps)
    ]
    unpick = jnp.concatenate(unpick, axis=0)
    width = share * rank
    low_column = iota((rows, width), 1).astype(F32)
    of_local = (low_column >= local * rank) & (low_column < (local + 1.0) * rank)
    of_local = jnp.where(of_local, 1.0, 0.0).astype(BF16)
    mask_out[...] = sum(dot(p, of_local) for p in pick).astype(BF16)

    pl.semaphore_wait(barrier, owners + tensors - 2)

    def exchange(out, into, send, recv, dest):
        return pltpu.make_async_remote_copy(
            src_ref=out.at[aligned(dest, chunk)],
            dst_ref=into.at[aligned(me, chunk)],
            send_sem=send.at[dest],
            recv_sem=recv.at[me],
            device_id={"replica": dest},
            device_id_type=MESH,
        )

    def arrival(out, into, send, recv, source):
        return pltpu.make_async_remote_copy(
            src_ref=out.at[aligned(source, chunk)],
            dst_ref=into.at[aligned(source, chunk)],
            send_sem=send.at[source],
            recv_sem=recv.at[source],
            device_id={"replica": source},
            device_id_type=MESH,
        )

    masks = (mask_out, mask_in, mask_send, mask_recv)
    placed = (heads_out, heads_in, heads_send, heads_recv)
    deltas = (delta_out, delta_in, delta_send, delta_recv)
    each(owners - 1, lambda i: exchange(*masks, ring(i + 1)).start())

    length = to_column(lengths_ref[...].astype(F32))
    every = cached + steps * rows
    place = iota((rows, every), 1).astype(F32)
    request = iota((rows, 1), 0).astype(F32)
    first = request * cache
    visible = (place >= first) & (place < first + length)
    allowed = []
    for s in range(steps):
        visible = visible | (place == request + (cached + s * rows))
        allowed.append(jnp.where(visible, 0.0, MASKED))
    bias = jnp.concatenate(allowed, axis=0)
    scale = 1.0 / math.sqrt(head)
    for load in loads[:5]:
        load.wait()
    for j in range(per_group):
        part = pl.ds(j * head, head)
        scores = dot_t(query[:, part], keys[...]) * scale
        scores = jnp.where(bias < 0.0, MASKED, scores)
        top = jnp.max(scores, axis=1, keepdims=True)
        weights = jnp.exp(scores - top)
        weights = (weights / jnp.sum(weights, axis=1, keepdims=True)).astype(BF16)
        heads[:, part] = dot(weights, values[...]).astype(BF16)

    mixed = heads[...]
    heads_out[...] = sum(
        dot(pick[s], mixed[s * rows : (s + 1) * rows]) for s in range(steps)
    ).astype(BF16)
    each(owners - 1, lambda i: exchange(*placed, ring(i + 1)).start())

    def low_copy(part, k):
        return pltpu.make_async_remote_copy(
            src_ref=low_out.at[part],
            dst_ref=low_in.at[mine, part],
            send_sem=low_send.at[part, peer(k)],
            recv_sem=low_recv.at[part, mine],
            device_id={"tensor": peer(k)},
            device_id_type=MESH,
        )

    def low_arrival(part, k):
        return pltpu.make_async_remote_copy(
            src_ref=low_out.at[part],
            dst_ref=low_in.at[peer(k), part],
            send_sem=low_send.at[part, peer(k)],
            recv_sem=low_recv.at[part, peer(k)],
            device_id={"tensor": peer(k)},
            device_id_type=MESH,
        )

    def lower(part, source_heads, source_mask):
        low = dot_t(source_heads[...], down[...]) * source_mask[...].astype(F32)
        low_out[part] = low.astype(BF16)
        for k in range(1, tensors):
            low_copy(part, k).start()

    loads[5].wait()
    own = aligned(me, chunk)
    lower(me, heads_out.at[own], mask_out.at[own])

    def base_copy(k):
        return pltpu.make_async_remote_copy(
            src_ref=base_out.at[k - 1],
            dst_ref=base_in.at[k - 1],
            send_sem=base_send.at[k - 1],
            recv_sem=base_recv.at[k - 1],
            device_id={"tensor": peer(k)},
            device_id_type=MESH,
        )

    loads[6].wait()
    for k in range(1, tensors):
        base_out[k - 1] = dot(mixed, matrix[:, aligned(peer(k), columns)]).astype(BF16)
        if k == 1:
            base_copy(k).start()
    base_own[...] = dot(mixed, matrix[:, aligned(mine, columns)])

    def lower_arrived(i):
        source = back(i + 1)
        here = aligned(source, chunk)
        arrival(*masks, source).wait_recv()
        arrival(*placed, source).wait_recv()
        lower(source, heads_in.at[here], mask_in.at[here])

    each(owners - 1, lower_arrived)
    for k in range(2, tensors):
        base_copy(k).start()

    def raise_back(part):
        low = low_out[part].astype(F32)
        for k in range(1, tensors):
            low_arrival(part, k).wait_recv()
            low = low + low_in[peer(k), part].astype(F32)
        return dot((ADAPTER_SCALE * low).astype(BF16), up[...]).astype(BF16)

    loads[7].wait()

    def raise_arrived(i):
        source = back(i + 1)
        delta_out[aligned(source, chunk)] = raise_back(source)
        exchange(*deltas, source).start()

    each(owners - 1, raise_arrived)
    delta_in[own] = raise_back(me)

    for k in range(1, tensors):
        base_copy(k).wait_recv()
        base_own[...] += base_in[k - 1].astype(F32)

    each(owners - 1, lambda i: arrival(*deltas, ring(i + 1)).wait_recv())
    delta = dot(unpick, delta_in[...])
    out_ref[...] = (base_own[...] + delta).astype(BF16)

    def sent(i):
        dest = ring(i + 1)
        exchange(*masks, dest).wait_send()
        exchange(*placed, dest).wait_send()
        exchange(*deltas, dest).wait_send()

    each(owners - 1, sent)

    def low_sent(part):
        for k in range(1, tensors):
            low_copy(part, k).wait_send()

    each(owners, low_sent)
    for k in range(1, tensors):
        base_copy(k).wait_send()


def per_device(
    owners,
    tensors,
    queries,
    key_cache,
    value_cache,
    decoded_keys,
    decoded_values,
    lengths,
    request_adapters,
    table_row_of,
    output_matrix,
    down_maps,
    up_maps,
):
    steps, rows, _, feature_width = queries.shape
    _, _, cache, head = key_cache.shape
    share, rank, columns = up_maps.shape
    cap = max(2, 2 * rows // owners)
    chunk = -(-max(16, steps * cap) // 16) * 16
    width = share * rank
    places = owners * chunk
    every = rows * cache + steps * rows
    down = jnp.swapaxes(down_maps.reshape(share, feature_width, rank), 1, 2)
    dma = pltpu.SemaphoreType.DMA
    vmem = pl.BlockSpec(memory_space=pltpu.VMEM)
    anywhere = pl.BlockSpec(memory_space=pl.ANY)
    dims = (steps, rows, cache, head, owners, tensors, share, rank, cap, chunk)
    out = pl.pallas_call(
        functools.partial(kernel, dims),
        name="decode_attention",
        out_shape=jax.ShapeDtypeStruct((steps * rows, columns), BF16),
        in_specs=[vmem] * 3 + [anywhere] * 8,
        out_specs=vmem,
        scratch_shapes=[
            pltpu.VMEM((steps * rows, feature_width), BF16),
            pltpu.VMEM((every, head), BF16),
            pltpu.VMEM((every, head), BF16),
            pltpu.VMEM(output_matrix.shape, BF16),
            pltpu.VMEM((width, feature_width), BF16),
            pltpu.VMEM((width, columns), BF16),
            pltpu.VMEM((steps * rows, feature_width), BF16),
            pltpu.VMEM((places, feature_width), BF16),
            pltpu.VMEM((places, feature_width), BF16),
            pltpu.VMEM((places, width), BF16),
            pltpu.VMEM((places, width), BF16),
            pltpu.VMEM((owners, chunk, width), BF16),
            pltpu.VMEM((tensors, owners, chunk, width), BF16),
            pltpu.VMEM((places, columns), BF16),
            pltpu.VMEM((places, columns), BF16),
            pltpu.VMEM((steps * rows, columns), F32),
            pltpu.VMEM((tensors - 1, steps * rows, columns), BF16),
            pltpu.VMEM((tensors - 1, steps * rows, columns), BF16),
            dma((8,)),
            dma((owners,)),
            dma((owners,)),
            dma((owners,)),
            dma((owners,)),
            dma((owners, tensors)),
            dma((owners, tensors)),
            dma((owners,)),
            dma((owners,)),
            dma((tensors - 1,)),
            dma((tensors - 1,)),
        ],
        compiler_params=pltpu.CompilerParams(
            collective_id=0, has_side_effects=True, vmem_limit_bytes=40 * 1024 * 1024
        ),
    )(
        lengths.reshape(1, rows),
        request_adapters.reshape(1, rows),
        table_row_of.reshape(1, -1),
        queries.reshape(steps * rows, feature_width),
        key_cache.reshape(rows * cache, head),
        value_cache.reshape(rows * cache, head),
        decoded_keys.reshape(steps * rows, head),
        decoded_values.reshape(steps * rows, head),
        output_matrix,
        down.reshape(width, feature_width),
        up_maps.reshape(width, columns),
    )
    return out.reshape(steps, rows, columns)


def solution(mesh):
    return jax.shard_map(
        functools.partial(per_device, mesh.shape["replica"], mesh.shape["tensor"]),
        mesh=mesh,
        in_specs=(
            P(None, ("groups", "replica"), "tensor", None),
            P(("groups", "replica"), "tensor", None, None),
            P(("groups", "replica"), "tensor", None, None),
            P(None, ("groups", "replica"), "tensor", None),
            P(None, ("groups", "replica"), "tensor", None),
            P(("groups", "replica")),
            P(("groups", "replica")),
            P("groups"),
            P("tensor", None),
            P("replica", "tensor", None, None),
            P("replica", None, "tensor"),
        ),
        out_specs=P(None, ("groups", "replica"), "tensor"),
        check_vma=False,
    )
```

```python
import functools
import math

import jax
import jax.numpy as jnp
from jax import lax
from jax.experimental import pallas as pl
from jax.experimental.pallas import tpu as pltpu
from jax.sharding import PartitionSpec as P

ADAPTER_SCALE = 2.0
MASKED = -1e30
MESH = pl.DeviceIdType.MESH
F32 = jnp.float32
BF16 = jnp.bfloat16


def iota(shape, dim):
    return lax.broadcasted_iota(jnp.int32, shape, dim)


def dot(a, b):
    return jnp.dot(a, b, preferred_element_type=F32)


def dot_t(a, b):
    return lax.dot_general(a, b, (((1,), (1,)), ((), ())), preferred_element_type=F32)


def aligned(start, size):
    return pl.ds(pl.multiple_of(start * size, size), size)


def to_column(row):
    n = row.shape[1]
    eye = iota((n, n), 0) == iota((n, n), 1)
    return jnp.sum(jnp.where(eye, row, 0.0), axis=1, keepdims=True)


def to_row(column):
    n = column.shape[0]
    eye = iota((n, n), 0) == iota((n, n), 1)
    return jnp.sum(jnp.where(eye, column, 0.0), axis=0, keepdims=True)


def each(count, body):
    if count <= 8:
        for i in range(count):
            body(i)
    else:
        lax.fori_loop(0, count, lambda i, c: (body(i), c)[1], 0)


def kernel(
    dims,
    lengths_hbm,
    adapters_hbm,
    table_hbm,
    query_hbm,
    key_hbm,
    value_hbm,
    new_key_hbm,
    new_value_hbm,
    matrix_hbm,
    down_hbm,
    up_hbm,
    out_ref,
    lengths_ref,
    adapters_ref,
    table_ref,
    query,
    keys,
    values,
    matrix,
    down,
    up,
    heads,
    heads_out,
    heads_in,
    mask_out,
    mask_in,
    low_out,
    low_in,
    delta_out,
    delta_in,
    base_own,
    base_out,
    base_in,
    local_sem,
    mask_send,
    mask_recv,
    heads_send,
    heads_recv,
    low_send,
    low_recv,
    delta_send,
    delta_recv,
    base_send,
    base_recv,
):
    steps, rows, cache, head, owners, tensors, share, rank, cap, chunk = dims
    me = lax.axis_index("replica")
    mine = lax.axis_index("tensor")
    columns = out_ref.shape[1]
    cached = rows * cache
    per_group = query.shape[1] // head

    def other(i):
        return lax.rem(me + 1 + i, owners)

    def peer(k):
        if tensors % 2:
            return lax.rem(mine + k, tensors)
        flipped = mine // 2 * 2 + (mine % 2 + k % 2) % 2
        return (flipped + k // 2 * 2) % tensors

    barrier = pltpu.get_barrier_semaphore()

    def greet(i):
        pl.semaphore_signal(
            barrier, inc=1, device_id={"replica": other(i)}, device_id_type=MESH
        )

    each(owners - 1, greet)
    for k in range(1, tensors):
        pl.semaphore_signal(barrier, inc=1, device_id={"tensor": peer(k)}, device_id_type=MESH)

    loads = [
        (adapters_hbm, adapters_ref),
        (table_hbm, table_ref),
        (lengths_hbm, lengths_ref),
        (query_hbm, query),
        (key_hbm, keys.at[pl.ds(0, cached)]),
        (new_key_hbm, keys.at[pl.ds(cached, steps * rows)]),
        (value_hbm, values.at[pl.ds(0, cached)]),
        (new_value_hbm, values.at[pl.ds(cached, steps * rows)]),
        (down_hbm, down),
        (matrix_hbm, matrix),
        (up_hbm, up),
    ]
    loads = [pltpu.make_async_copy(a, b, local_sem.at[i]) for i, (a, b) in enumerate(loads)]
    for load in loads:
        load.start()

    for load in loads[:2]:
        load.wait()

    wanted = to_column(adapters_ref[...].astype(F32))
    total = table_ref.shape[1]
    hit = wanted == iota((rows, total), 1).astype(F32)
    stored = jnp.sum(jnp.where(hit, table_ref[...].astype(F32), 0.0), axis=1, keepdims=True)
    owner = jnp.floor((stored + 0.5) / share)
    local = stored - owner * share
    owner_row = to_row(owner)
    earlier = iota((rows, rows), 1) < iota((rows, rows), 0)
    rank_in = jnp.sum(
        jnp.where(earlier & (owner == owner_row), 1.0, 0.0), axis=1, keepdims=True
    )
    slot = owner * chunk + rank_in
    slot_row = to_row(slot)
    places = owners * chunk
    place_row = iota((places, rows), 0).astype(F32)
    place_col = iota((rows, places), 1).astype(F32)
    pick = [
        jnp.where(place_row == slot_row + s * cap, 1.0, 0.0).astype(BF16) for s in range(steps)
    ]
    unpick = [
        jnp.where(place_col == slot + s * cap, 1.0, 0.0).astype(BF16) for s in range(steps)
    ]
    unpick = jnp.concatenate(unpick, axis=0)
    width = share * rank
    low_column = iota((rows, width), 1).astype(F32)
    of_local = (low_column >= local * rank) & (low_column < (local + 1.0) * rank)
    of_local = jnp.where(of_local, 1.0, 0.0).astype(BF16)
    mask_out[...] = sum(dot(p, of_local) for p in pick).astype(BF16)

    def exchange(out, into, send, recv, dest):
        return pltpu.make_async_remote_copy(
            src_ref=out.at[aligned(dest, chunk)],
            dst_ref=into.at[aligned(me, chunk)],
            send_sem=send.at[dest],
            recv_sem=recv.at[me],
            device_id={"replica": dest},
            device_id_type=MESH,
        )

    def arrival(out, into, send, recv, source):
        return pltpu.make_async_remote_copy(
            src_ref=out.at[aligned(source, chunk)],
            dst_ref=into.at[aligned(source, chunk)],
            send_sem=send.at[source],
            recv_sem=recv.at[source],
            device_id={"replica": source},
            device_id_type=MESH,
        )

    masks = (mask_out, mask_in, mask_send, mask_recv)
    placed = (heads_out, heads_in, heads_send, heads_recv)
    deltas = (delta_out, delta_in, delta_send, delta_recv)

    loads[2].wait()
    length = to_column(lengths_ref[...].astype(F32))
    every = cached + steps * rows
    place = iota((rows, every), 1).astype(F32)
    request = iota((rows, 1), 0).astype(F32)
    first = request * cache
    visible = (place >= first) & (place < first + length)
    allowed = []
    for s in range(steps):
        visible = visible | (place == request + (cached + s * rows))
        allowed.append(jnp.where(visible, 0.0, MASKED))
    bias = jnp.concatenate(allowed, axis=0)
    scale = 1.0 / math.sqrt(head)
    for load in loads[3:8]:
        load.wait()
    for j in range(per_group):
        part = pl.ds(j * head, head)
        scores = dot_t(query[:, part], keys[...]) * scale
        scores = jnp.where(bias < 0.0, MASKED, scores)
        top = jnp.max(scores, axis=1, keepdims=True)
        weights = jnp.exp(scores - top)
        weights = (weights / jnp.sum(weights, axis=1, keepdims=True)).astype(BF16)
        heads[:, part] = dot(weights, values[...]).astype(BF16)

    mixed = heads[...]
    heads_out[...] = sum(
        dot(pick[s], mixed[s * rows : (s + 1) * rows]) for s in range(steps)
    ).astype(BF16)
    def base_copy(k):
        return pltpu.make_async_remote_copy(
            src_ref=base_out.at[k - 1],
            dst_ref=base_in.at[k - 1],
            send_sem=base_send.at[k - 1],
            recv_sem=base_recv.at[k - 1],
            device_id={"tensor": peer(k)},
            device_id_type=MESH,
        )

    pl.semaphore_wait(barrier, owners + tensors - 2)
    each(owners - 1, lambda i: exchange(*masks, other(i)).start())
    each(owners - 1, lambda i: exchange(*placed, other(i)).start())

    def low_copy(part, k):
        return pltpu.make_async_remote_copy(
            src_ref=low_out.at[part],
            dst_ref=low_in.at[mine, part],
            send_sem=low_send.at[part, peer(k)],
            recv_sem=low_recv.at[part, mine],
            device_id={"tensor": peer(k)},
            device_id_type=MESH,
        )

    def low_arrival(part, k):
        return pltpu.make_async_remote_copy(
            src_ref=low_out.at[part],
            dst_ref=low_in.at[peer(k), part],
            send_sem=low_send.at[part, peer(k)],
            recv_sem=low_recv.at[part, peer(k)],
            device_id={"tensor": peer(k)},
            device_id_type=MESH,
        )

    def lower(part, source_heads, source_mask):
        low = dot_t(source_heads[...], down[...]) * source_mask[...].astype(F32)
        low_out[part] = low.astype(BF16)
        for k in range(1, tensors):
            low_copy(part, k).start()

    loads[8].wait()
    own = aligned(me, chunk)
    lower(me, heads_out.at[own], mask_out.at[own])

    loads[9].wait()
    for k in range(1, tensors):
        base_out[k - 1] = dot(mixed, matrix[:, aligned(peer(k), columns)]).astype(BF16)
    base_own[...] = dot(mixed, matrix[:, aligned(mine, columns)])

    for k in range(1, tensors - 1):
        base_copy(k).start()

    def lower_arrived(i):
        source = other(i)
        here = aligned(source, chunk)
        arrival(*masks, source).wait_recv()
        arrival(*placed, source).wait_recv()
        lower(source, heads_in.at[here], mask_in.at[here])

    each(owners - 1, lower_arrived)
    base_copy(tensors - 1).start()

    def raise_back(part):
        low = low_out[part].astype(F32)
        for k in range(1, tensors):
            low_arrival(part, k).wait_recv()
            low = low + low_in[peer(k), part].astype(F32)
        return dot((ADAPTER_SCALE * low).astype(BF16), up[...]).astype(BF16)

    loads[10].wait()

    def raise_arrived(i):
        source = other(i)
        delta_out[aligned(source, chunk)] = raise_back(source)
        exchange(*deltas, source).start()

    each(owners - 1, raise_arrived)
    delta_in[own] = raise_back(me)

    for k in range(1, tensors):
        base_copy(k).wait_recv()
        base_own[...] += base_in[k - 1].astype(F32)

    each(owners - 1, lambda i: arrival(*deltas, other(i)).wait_recv())
    delta = dot(unpick, delta_in[...])
    out_ref[...] = (base_own[...] + delta).astype(BF16)

    def sent(i):
        dest = other(i)
        exchange(*masks, dest).wait_send()
        exchange(*placed, dest).wait_send()
        exchange(*deltas, dest).wait_send()

    each(owners - 1, sent)

    def low_sent(part):
        for k in range(1, tensors):
            low_copy(part, k).wait_send()

    each(owners, low_sent)
    for k in range(1, tensors):
        base_copy(k).wait_send()


def per_device(
    owners,
    tensors,
    queries,
    key_cache,
    value_cache,
    decoded_keys,
    decoded_values,
    lengths,
    request_adapters,
    table_row_of,
    output_matrix,
    down_maps,
    up_maps,
):
    steps, rows, _, feature_width = queries.shape
    _, _, cache, head = key_cache.shape
    share, rank, columns = up_maps.shape
    cap = max(2, 2 * rows // owners)
    chunk = -(-max(16, steps * cap) // 16) * 16
    width = share * rank
    places = owners * chunk
    every = rows * cache + steps * rows
    down = jnp.swapaxes(down_maps.reshape(share, feature_width, rank), 1, 2)
    dma = pltpu.SemaphoreType.DMA
    vmem = pl.BlockSpec(memory_space=pltpu.VMEM)
    hbm = pl.BlockSpec(memory_space=pltpu.HBM)
    dims = (steps, rows, cache, head, owners, tensors, share, rank, cap, chunk)
    out = pl.pallas_call(
        functools.partial(kernel, dims),
        name="decode_attention",
        out_shape=jax.ShapeDtypeStruct((steps * rows, columns), BF16),
        in_specs=[hbm] * 11,
        out_specs=vmem,
        scratch_shapes=[
            pltpu.VMEM((1, rows), jnp.int32),
            pltpu.VMEM((1, rows), jnp.int32),
            pltpu.VMEM((1, table_row_of.shape[0]), jnp.int32),
            pltpu.VMEM((steps * rows, feature_width), BF16),
            pltpu.VMEM((every, head), BF16),
            pltpu.VMEM((every, head), BF16),
            pltpu.VMEM(output_matrix.shape, BF16),
            pltpu.VMEM((width, feature_width), BF16),
            pltpu.VMEM((width, columns), BF16),
            pltpu.VMEM((steps * rows, feature_width), BF16),
            pltpu.VMEM((places, feature_width), BF16),
            pltpu.VMEM((places, feature_width), BF16),
            pltpu.VMEM((places, width), BF16),
            pltpu.VMEM((places, width), BF16),
            pltpu.VMEM((owners, chunk, width), BF16),
            pltpu.VMEM((tensors, owners, chunk, width), BF16),
            pltpu.VMEM((places, columns), BF16),
            pltpu.VMEM((places, columns), BF16),
            pltpu.VMEM((steps * rows, columns), F32),
            pltpu.VMEM((tensors - 1, steps * rows, columns), BF16),
            pltpu.VMEM((tensors - 1, steps * rows, columns), BF16),
            dma((11,)),
            dma((owners,)),
            dma((owners,)),
            dma((owners,)),
            dma((owners,)),
            dma((owners, tensors)),
            dma((owners, tensors)),
            dma((owners,)),
            dma((owners,)),
            dma((tensors - 1,)),
            dma((tensors - 1,)),
        ],
        compiler_params=pltpu.CompilerParams(
            collective_id=0, has_side_effects=True, vmem_limit_bytes=63 * 1024 * 1024
        ),
    )(
        lengths.reshape(1, rows),
        request_adapters.reshape(1, rows),
        table_row_of.reshape(1, -1),
        queries.reshape(steps * rows, feature_width),
        key_cache.reshape(rows * cache, head),
        value_cache.reshape(rows * cache, head),
        decoded_keys.reshape(steps * rows, head),
        decoded_values.reshape(steps * rows, head),
        output_matrix,
        down.reshape(width, feature_width),
        up_maps.reshape(width, columns),
    )
    return out.reshape(steps, rows, columns)


def solution(mesh):
    return jax.shard_map(
        functools.partial(per_device, mesh.shape["replica"], mesh.shape["tensor"]),
        mesh=mesh,
        in_specs=(
            P(None, ("groups", "replica"), "tensor", None),
            P(("groups", "replica"), "tensor", None, None),
            P(("groups", "replica"), "tensor", None, None),
            P(None, ("groups", "replica"), "tensor", None),
            P(None, ("groups", "replica"), "tensor", None),
            P(("groups", "replica")),
            P(("groups", "replica")),
            P("groups"),
            P("tensor", None),
            P("replica", "tensor", None, None),
            P("replica", None, "tensor"),
        ),
        out_specs=P(None, ("groups", "replica"), "tensor"),
        check_vma=False,
    )
```

```python
import functools
import math

import jax
import jax.numpy as jnp
from jax import lax
from jax.experimental import pallas as pl
from jax.experimental.pallas import tpu as pltpu
from jax.sharding import PartitionSpec as P

ADAPTER_SCALE = 2.0
MASKED = -1e30
MESH = pl.DeviceIdType.MESH
F32 = jnp.float32
BF16 = jnp.bfloat16


def iota(shape, dim):
    return lax.broadcasted_iota(jnp.int32, shape, dim)


def dot(a, b):
    return jnp.dot(a, b, preferred_element_type=F32)


def dot_t(a, b):
    return lax.dot_general(a, b, (((1,), (1,)), ((), ())), preferred_element_type=F32)


def aligned(start, size):
    return pl.ds(pl.multiple_of(start * size, size), size)


def to_column(row):
    n = row.shape[1]
    eye = iota((n, n), 0) == iota((n, n), 1)
    return jnp.sum(jnp.where(eye, row, 0.0), axis=1, keepdims=True)


def to_row(column):
    n = column.shape[0]
    eye = iota((n, n), 0) == iota((n, n), 1)
    return jnp.sum(jnp.where(eye, column, 0.0), axis=0, keepdims=True)


def each(count, body):
    if count <= 8:
        for i in range(count):
            body(i)
    else:
        lax.fori_loop(0, count, lambda i, c: (body(i), c)[1], 0)


def kernel(
    dims,
    lengths_hbm,
    adapters_hbm,
    table_hbm,
    query_hbm,
    key_hbm,
    value_hbm,
    new_key_hbm,
    new_value_hbm,
    matrix_hbm,
    down_hbm,
    up_hbm,
    out_ref,
    lengths_ref,
    adapters_ref,
    table_ref,
    query,
    keys,
    values,
    matrix,
    down,
    up,
    heads,
    heads_out,
    heads_in,
    mask_out,
    mask_in,
    low_out,
    low_in,
    delta_out,
    delta_in,
    base_own,
    base_out,
    base_in,
    local_sem,
    mask_send,
    mask_recv,
    heads_send,
    heads_recv,
    low_send,
    low_recv,
    delta_send,
    delta_recv,
    base_send,
    base_recv,
):
    steps, rows, cache, head, owners, tensors, share, rank, cap, chunk = dims
    me = lax.axis_index("replica")
    mine = lax.axis_index("tensor")
    columns = out_ref.shape[1]
    cached = rows * cache
    per_group = query.shape[1] // head

    def other(i):
        return lax.rem(me + 1 + i, owners)

    def peer(k):
        if tensors % 2:
            return lax.rem(mine + k, tensors)
        flipped = mine // 2 * 2 + (mine % 2 + k % 2) % 2
        return (flipped + k // 2 * 2) % tensors

    barrier = pltpu.get_barrier_semaphore()

    def greet(i):
        pl.semaphore_signal(
            barrier, inc=1, device_id={"replica": other(i)}, device_id_type=MESH
        )

    each(owners - 1, greet)
    for k in range(1, tensors):
        pl.semaphore_signal(barrier, inc=1, device_id={"tensor": peer(k)}, device_id_type=MESH)

    loads = [
        (adapters_hbm, adapters_ref),
        (table_hbm, table_ref),
        (lengths_hbm, lengths_ref),
        (query_hbm, query),
        (key_hbm, keys.at[pl.ds(0, cached)]),
        (new_key_hbm, keys.at[pl.ds(cached, steps * rows)]),
        (value_hbm, values.at[pl.ds(0, cached)]),
        (new_value_hbm, values.at[pl.ds(cached, steps * rows)]),
        (down_hbm, down),
        (matrix_hbm, matrix),
        (up_hbm, up),
    ]
    loads = [pltpu.make_async_copy(a, b, local_sem.at[i]) for i, (a, b) in enumerate(loads)]
    for load in loads:
        load.start()

    for load in loads[:2]:
        load.wait()

    wanted = to_column(adapters_ref[...].astype(F32))
    total = table_ref.shape[1]
    hit = wanted == iota((rows, total), 1).astype(F32)
    stored = jnp.sum(jnp.where(hit, table_ref[...].astype(F32), 0.0), axis=1, keepdims=True)
    owner = jnp.floor((stored + 0.5) / share)
    local = stored - owner * share
    owner_row = to_row(owner)
    earlier = iota((rows, rows), 1) < iota((rows, rows), 0)
    rank_in = jnp.sum(
        jnp.where(earlier & (owner == owner_row), 1.0, 0.0), axis=1, keepdims=True
    )
    slot = owner * chunk + rank_in
    slot_row = to_row(slot)
    places = owners * chunk
    place_row = iota((places, rows), 0).astype(F32)
    place_col = iota((rows, places), 1).astype(F32)
    pick = [
        jnp.where(place_row == slot_row + s * cap, 1.0, 0.0).astype(BF16) for s in range(steps)
    ]
    unpick = [
        jnp.where(place_col == slot + s * cap, 1.0, 0.0).astype(BF16) for s in range(steps)
    ]
    unpick = jnp.concatenate(unpick, axis=0)
    taken = sum(jnp.where(place_col == slot + s * cap, local + 1.0, 0.0) for s in range(steps))
    mask_out[0] = jnp.sum(taken, axis=0, keepdims=True) - 1.0

    def exchange(out, into, send, recv, dest):
        return pltpu.make_async_remote_copy(
            src_ref=out.at[aligned(dest, chunk)],
            dst_ref=into.at[aligned(me, chunk)],
            send_sem=send.at[dest],
            recv_sem=recv.at[me],
            device_id={"replica": dest},
            device_id_type=MESH,
        )

    def arrival(out, into, send, recv, source):
        return pltpu.make_async_remote_copy(
            src_ref=out.at[aligned(source, chunk)],
            dst_ref=into.at[aligned(source, chunk)],
            send_sem=send.at[source],
            recv_sem=recv.at[source],
            device_id={"replica": source},
            device_id_type=MESH,
        )

    def mask_copy(dest):
        return pltpu.make_async_remote_copy(
            src_ref=mask_out.at[0],
            dst_ref=mask_in.at[me],
            send_sem=mask_send.at[dest],
            recv_sem=mask_recv.at[me],
            device_id={"replica": dest},
            device_id_type=MESH,
        )

    def mask_arrival(source):
        return pltpu.make_async_remote_copy(
            src_ref=mask_out.at[0],
            dst_ref=mask_in.at[source],
            send_sem=mask_send.at[source],
            recv_sem=mask_recv.at[source],
            device_id={"replica": source},
            device_id_type=MESH,
        )

    placed = (heads_out, heads_in, heads_send, heads_recv)
    deltas = (delta_out, delta_in, delta_send, delta_recv)

    loads[2].wait()
    length = to_column(lengths_ref[...].astype(F32))
    every = cached + steps * rows
    place = iota((rows, every), 1).astype(F32)
    request = iota((rows, 1), 0).astype(F32)
    first = request * cache
    visible = (place >= first) & (place < first + length)
    allowed = []
    for s in range(steps):
        visible = visible | (place == request + (cached + s * rows))
        allowed.append(jnp.where(visible, 0.0, MASKED))
    bias = jnp.concatenate(allowed, axis=0)
    scale = 1.0 / math.sqrt(head)
    for load in loads[3:8]:
        load.wait()
    for j in range(per_group):
        part = pl.ds(j * head, head)
        scores = dot_t(query[:, part], keys[...]) * scale
        scores = jnp.where(bias < 0.0, MASKED, scores)
        top = jnp.max(scores, axis=1, keepdims=True)
        weights = jnp.exp(scores - top)
        weights = (weights / jnp.sum(weights, axis=1, keepdims=True)).astype(BF16)
        heads[:, part] = dot(weights, values[...]).astype(BF16)

    mixed = heads[...]
    heads_out[...] = sum(
        dot(pick[s], mixed[s * rows : (s + 1) * rows]) for s in range(steps)
    ).astype(BF16)
    def base_copy(k):
        return pltpu.make_async_remote_copy(
            src_ref=base_out.at[k - 1],
            dst_ref=base_in.at[k - 1],
            send_sem=base_send.at[k - 1],
            recv_sem=base_recv.at[k - 1],
            device_id={"tensor": peer(k)},
            device_id_type=MESH,
        )

    pl.semaphore_wait(barrier, owners + tensors - 2)
    each(owners - 1, lambda i: mask_copy(other(i)).start())
    each(owners - 1, lambda i: exchange(*placed, other(i)).start())

    def low_copy(part, k):
        return pltpu.make_async_remote_copy(
            src_ref=low_out.at[part],
            dst_ref=low_in.at[mine, part],
            send_sem=low_send.at[part, peer(k)],
            recv_sem=low_recv.at[part, mine],
            device_id={"tensor": peer(k)},
            device_id_type=MESH,
        )

    def low_arrival(part, k):
        return pltpu.make_async_remote_copy(
            src_ref=low_out.at[part],
            dst_ref=low_in.at[peer(k), part],
            send_sem=low_send.at[part, peer(k)],
            recv_sem=low_recv.at[part, peer(k)],
            device_id={"tensor": peer(k)},
            device_id_type=MESH,
        )

    width = share * rank

    def lower(part, source_heads, locals_row):
        here = iota((chunk, places), 1) == iota((chunk, places), 0) + me * chunk
        first = rank * jnp.sum(jnp.where(here, locals_row, 0.0), axis=1, keepdims=True)
        column = iota((chunk, width), 1).astype(F32)
        of_row = (column >= first) & (column < first + rank)
        low = jnp.where(of_row, dot_t(source_heads[...], down[...]), 0.0)
        low_out[part] = low.astype(BF16)
        for k in range(1, tensors):
            low_copy(part, k).start()

    loads[8].wait()
    own = aligned(me, chunk)
    lower(me, heads_out.at[own], mask_out[0])

    loads[9].wait()
    for k in range(1, tensors):
        base_out[k - 1] = dot(mixed, matrix[:, aligned(peer(k), columns)]).astype(BF16)
    base_own[...] = dot(mixed, matrix[:, aligned(mine, columns)])

    for k in range(1, tensors - 1):
        base_copy(k).start()

    def lower_arrived(i):
        source = other(i)
        here = aligned(source, chunk)
        mask_arrival(source).wait_recv()
        arrival(*placed, source).wait_recv()
        lower(source, heads_in.at[here], mask_in[source])

    each(owners - 1, lower_arrived)
    base_copy(tensors - 1).start()

    def raise_back(part):
        low = low_out[part].astype(F32)
        for k in range(1, tensors):
            low_arrival(part, k).wait_recv()
            low = low + low_in[peer(k), part].astype(F32)
        return dot((ADAPTER_SCALE * low).astype(BF16), up[...]).astype(BF16)

    loads[10].wait()

    def raise_arrived(i):
        source = other(i)
        delta_out[aligned(source, chunk)] = raise_back(source)
        exchange(*deltas, source).start()

    each(owners - 1, raise_arrived)
    delta_in[own] = raise_back(me)

    for k in range(1, tensors):
        base_copy(k).wait_recv()
        base_own[...] += base_in[k - 1].astype(F32)

    each(owners - 1, lambda i: arrival(*deltas, other(i)).wait_recv())
    delta = dot(unpick, delta_in[...])
    out_ref[...] = (base_own[...] + delta).astype(BF16)

    def sent(i):
        dest = other(i)
        mask_copy(dest).wait_send()
        exchange(*placed, dest).wait_send()
        exchange(*deltas, dest).wait_send()

    each(owners - 1, sent)

    def low_sent(part):
        for k in range(1, tensors):
            low_copy(part, k).wait_send()

    each(owners, low_sent)
    for k in range(1, tensors):
        base_copy(k).wait_send()


def per_device(
    owners,
    tensors,
    queries,
    key_cache,
    value_cache,
    decoded_keys,
    decoded_values,
    lengths,
    request_adapters,
    table_row_of,
    output_matrix,
    down_maps,
    up_maps,
):
    steps, rows, _, feature_width = queries.shape
    _, _, cache, head = key_cache.shape
    share, rank, columns = up_maps.shape
    cap = max(2, 2 * rows // owners)
    chunk = -(-max(16, steps * cap) // 16) * 16
    width = share * rank
    places = owners * chunk
    every = rows * cache + steps * rows
    down = jnp.swapaxes(down_maps.reshape(share, feature_width, rank), 1, 2)
    dma = pltpu.SemaphoreType.DMA
    vmem = pl.BlockSpec(memory_space=pltpu.VMEM)
    hbm = pl.BlockSpec(memory_space=pltpu.HBM)
    dims = (steps, rows, cache, head, owners, tensors, share, rank, cap, chunk)
    out = pl.pallas_call(
        functools.partial(kernel, dims),
        name="decode_attention",
        out_shape=jax.ShapeDtypeStruct((steps * rows, columns), BF16),
        in_specs=[hbm] * 11,
        out_specs=vmem,
        scratch_shapes=[
            pltpu.VMEM((1, rows), jnp.int32),
            pltpu.VMEM((1, rows), jnp.int32),
            pltpu.VMEM((1, table_row_of.shape[0]), jnp.int32),
            pltpu.VMEM((steps * rows, feature_width), BF16),
            pltpu.VMEM((every, head), BF16),
            pltpu.VMEM((every, head), BF16),
            pltpu.VMEM(output_matrix.shape, BF16),
            pltpu.VMEM((width, feature_width), BF16),
            pltpu.VMEM((width, columns), BF16),
            pltpu.VMEM((steps * rows, feature_width), BF16),
            pltpu.VMEM((places, feature_width), BF16),
            pltpu.VMEM((places, feature_width), BF16),
            pltpu.VMEM((1, 1, places), F32),
            pltpu.VMEM((owners, 1, places), F32),
            pltpu.VMEM((owners, chunk, width), BF16),
            pltpu.VMEM((tensors, owners, chunk, width), BF16),
            pltpu.VMEM((places, columns), BF16),
            pltpu.VMEM((places, columns), BF16),
            pltpu.VMEM((steps * rows, columns), F32),
            pltpu.VMEM((tensors - 1, steps * rows, columns), BF16),
            pltpu.VMEM((tensors - 1, steps * rows, columns), BF16),
            dma((11,)),
            dma((owners,)),
            dma((owners,)),
            dma((owners,)),
            dma((owners,)),
            dma((owners, tensors)),
            dma((owners, tensors)),
            dma((owners,)),
            dma((owners,)),
            dma((tensors - 1,)),
            dma((tensors - 1,)),
        ],
        compiler_params=pltpu.CompilerParams(
            collective_id=0, has_side_effects=True, vmem_limit_bytes=63 * 1024 * 1024
        ),
    )(
        lengths.reshape(1, rows),
        request_adapters.reshape(1, rows),
        table_row_of.reshape(1, -1),
        queries.reshape(steps * rows, feature_width),
        key_cache.reshape(rows * cache, head),
        value_cache.reshape(rows * cache, head),
        decoded_keys.reshape(steps * rows, head),
        decoded_values.reshape(steps * rows, head),
        output_matrix,
        down.reshape(width, feature_width),
        up_maps.reshape(width, columns),
    )
    return out.reshape(steps, rows, columns)


def solution(mesh):
    return jax.shard_map(
        functools.partial(per_device, mesh.shape["replica"], mesh.shape["tensor"]),
        mesh=mesh,
        in_specs=(
            P(None, ("groups", "replica"), "tensor", None),
            P(("groups", "replica"), "tensor", None, None),
            P(("groups", "replica"), "tensor", None, None),
            P(None, ("groups", "replica"), "tensor", None),
            P(None, ("groups", "replica"), "tensor", None),
            P(("groups", "replica")),
            P(("groups", "replica")),
            P("groups"),
            P("tensor", None),
            P("replica", "tensor", None, None),
            P("replica", None, "tensor"),
        ),
        out_specs=P(None, ("groups", "replica"), "tensor"),
        check_vma=False,
    )
```
